256 devices in a mesh: dp: 2 (over y_hi), row: 8 (over x, y_lo), col: 16 (over z, core).
Axes of the slice: x: 4, y: 4 (y_hi: 2, y_lo: 2; y = y_hi * 2 + y_lo), z: 8, core: 2. Of those that a mesh axis runs over, the one named last changes fastest.
Arguments:
- view_a: bfloat16 [256, 32768], P('dp', ('row', 'col')), may hold values from -22 to 22
- view_b: bfloat16 [256, 32768], P('dp', ('row', 'col')), may hold values from -22 to 22
Outputs:
- grad_a: float32 [256, 32768], P('dp', ('row', 'col'))
- grad_b: float32 [256, 32768], P('dp', ('row', 'col'))
- objective: float32 [], replicated
The draws below stay inside these ranges and needn't reach their ends.
All inputs are finite; a program needn't handle non-finite values.
Results may differ from the reference program's by a relative error of at most 0.0028.
Values may be sent and summed in bfloat16 or wider, within the bound.
No kernel may reach another device: no remote copies, remote signals or barrier semaphores. Data moves between devices by JAX's collectives and lax.ppermute only.
A program may use at most 64 MiB of HBM per device.

```python
import math
import jax
import jax.numpy as jnp
from jax import lax

F = 32768
N = 256


def shared_parts(key):
    keys = jax.random.split(jax.random.fold_in(key, 11), 4)
    pick = jax.random.randint(keys[0], (F,), 0, 2)
    low_part = jax.random.uniform(keys[1], (F,), jnp.float32, -1.6, -0.7)
    high_part = jax.random.uniform(keys[2], (F,), jnp.float32, 0.7, 1.2)
    scale = jnp.exp(jnp.where(pick == 1, high_part, low_part))
    offset = jax.random.uniform(keys[3], (F,), jnp.float32, -1.0, 1.0)
    return (scale, offset)


def rough(key):
    first = jax.random.fold_in(key, 0)
    normal_part = jax.random.truncated_normal(first, -4.0, 4.0, (N, F), jnp.float32)
    return normal_part


def build_view(key, own_key):
    scale, offset = shared_parts(key)
    common = rough(jax.random.fold_in(key, 21))
    own = rough(own_key)
    value = scale * (offset + (common + 0.5 * own) / math.sqrt(1.25))
    return value.astype(jnp.bfloat16)


def draw_view_a(key, part):
    own_key = jax.random.fold_in(key, 1)
    return build_view(key, own_key)


def draw_view_b(key, part):
    own_key = jax.random.fold_in(key, 2)
    return build_view(key, own_key)


def setup_inputs(seed: int = 0) -> dict:
    arg_keys = jax.random.split(jax.random.key(seed), 3)
    return {
        "view_a": draw_view_a(jax.random.fold_in(arg_keys[2], 71), 0),
        "view_b": draw_view_b(jax.random.fold_in(arg_keys[2], 71), 0),
    }


def view_terms(z):
    zf = z.astype(jnp.float32)
    mean = lax.optimization_barrier(jnp.mean(zf, axis=0))
    diff = zf - mean
    std = jnp.sqrt(lax.optimization_barrier(jnp.sum(diff * diff, axis=0)) / (N - 1) + 0.0001)
    centered = diff.astype(jnp.bfloat16)
    block = min(1024, F)
    col_ids = jnp.arange(F, dtype=jnp.int32)

    def step(carry, index):
        pull, square = carry
        start = (index * block).astype(jnp.int32)
        rows = lax.dynamic_slice_in_dim(centered, start, block, 1)
        cov = lax.dot_general(rows, centered, (((0,), (0,)), ((), ())), preferred_element_type=jnp.float32) / (N - 1)
        row_ids = start + jnp.arange(block, dtype=jnp.int32)
        off = jnp.where(row_ids[:, None] == col_ids[None, :], jnp.float32(0.0), cov)
        square = square + jnp.sum(off * off)
        pull = pull + jnp.dot(rows.astype(jnp.float32), off, preferred_element_type=jnp.float32, precision=lax.Precision.HIGHEST)
        return ((pull, square), None)
    init = (jnp.zeros((N, F), jnp.float32), jnp.zeros((), jnp.float32))
    (pull, square), unused = lax.scan(step, init, jnp.arange(F // block, dtype=jnp.int32))
    return (diff, std, pull, square)

def reference(view_a, view_b):
    diff_a, std_a, pull_a, square_a = view_terms(view_a)
    diff_b, std_b, pull_b, square_b = view_terms(view_b)
    gap = view_a.astype(jnp.float32) - view_b.astype(jnp.float32)
    coef = 2.0 * N / (25.0 * (N - 1))
    hinge_a = jnp.where(std_a < 1.0, N * diff_a / (2.0 * std_a * (N - 1)), jnp.float32(0.0))
    hinge_b = jnp.where(std_b < 1.0, N * diff_b / (2.0 * std_b * (N - 1)), jnp.float32(0.0))
    grad_a = gap - hinge_a + coef * (pull_a - lax.optimization_barrier(jnp.mean(pull_a, axis=0)))
    grad_b = -gap - hinge_b + coef * (pull_b - lax.optimization_barrier(jnp.mean(pull_b, axis=0)))
    loss = 25.0 * jnp.sum(gap * gap) / (N * F)
    loss = loss + 25.0 * (jnp.sum(jnp.maximum(1.0 - std_a, 0.0)) + jnp.sum(jnp.maximum(1.0 - std_b, 0.0))) / F
    loss = loss + (square_a + square_b) / F
    objective = loss * N / (50.0 * F)
    return (grad_a, grad_b, objective)
```

```python
import jax
import jax.numpy as jnp
from jax import lax
from jax.experimental import pallas as pl
from jax.experimental.pallas import tpu as pltpu
from jax.sharding import Mesh, PartitionSpec as P

AXES = ("dp", "x", "yl", "z", "core")
CHIPS = ("x", "yl", "z")
TILE_R, TILE_C = 8, 128


def split3(value):
    first = value.astype(jnp.bfloat16)
    rest = value - first.astype(jnp.float32)
    second = rest.astype(jnp.bfloat16)
    third = (rest - second.astype(jnp.float32)).astype(jnp.bfloat16)
    return (first, second, third)


def place(tile, row, col, scalar):
    rows = lax.broadcasted_iota(jnp.int32, tile.shape, 0)
    cols = lax.broadcasted_iota(jnp.int32, tile.shape, 1)
    return jnp.where((rows == row) & (cols == col), scalar, tile)


def pick(tile, row, col):
    rows = lax.broadcasted_iota(jnp.int32, tile.shape, 0)
    cols = lax.broadcasted_iota(jnp.int32, tile.shape, 1)
    kept = jnp.where((rows == row) & (cols == col), tile, jnp.float32(0.0))
    return jnp.sum(kept, axis=(0, 1), keepdims=True)


def total_sum(value):
    return jnp.sum(value, axis=(0, 1), keepdims=True)


def gram_kernel(n_all, f_all, own_a, own_b, far, tiles, cent_a, cent_b, base_a, base_b):
    n_dev = own_a.shape[0]
    coef = 2.0 * n_all / (25.0 * (n_all - 1))
    near = (own_a[...].astype(jnp.float32), own_b[...].astype(jnp.float32))
    other = (far[0].astype(jnp.float32), far[1].astype(jnp.float32))
    gap = near[0] - near[1]
    gap_far = other[0] - other[1]
    common = (25.0 / (n_all * f_all)) * (total_sum(gap * gap) + total_sum(gap_far * gap_far))
    grams = []
    for view, (cent, base) in enumerate(((cent_a, base_a), (cent_b, base_b))):
        mine, theirs = near[view], other[view]
        mean = (
            jnp.sum(mine, axis=0, keepdims=True) + jnp.sum(theirs, axis=0, keepdims=True)
        ) / n_all
        diff, diff_far = mine - mean, theirs - mean
        squares = jnp.sum(diff * diff, axis=0, keepdims=True) + jnp.sum(
            diff_far * diff_far, axis=0, keepdims=True
        )
        std = jnp.sqrt(squares / (n_all - 1) + 0.0001)
        c_near, c_far = diff.astype(jnp.bfloat16), diff_far.astype(jnp.bfloat16)
        cent[:n_dev] = c_near
        cent[n_dev:] = c_far
        f_near, f_far = c_near.astype(jnp.float32), c_far.astype(jnp.float32)
        r = jnp.sum(f_near, axis=0, keepdims=True) + jnp.sum(f_far, axis=0, keepdims=True)
        d = (
            jnp.sum(f_near * f_near, axis=0, keepdims=True)
            + jnp.sum(f_far * f_far, axis=0, keepdims=True)
        ) / (n_all - 1)
        hinge = jnp.where(std < 1.0, n_all / (2.0 * std * (n_all - 1)), jnp.float32(0.0))
        sign = 1.0 if view == 0 else -1.0
        base[...] = sign * gap - hinge * diff - coef * (d * (f_near - r / n_all))
        common = common + (25.0 / f_all) * total_sum(jnp.maximum(1.0 - std, 0.0))
        common = common - total_sum(d * d) / f_all
        every = jnp.concatenate([c_near, c_far], axis=0)
        dims = (((1,), (1,)), ((), ()))
        r1, r2, r3 = split3(r)
        rows16 = lax.broadcasted_iota(jnp.int32, (16, r.shape[1]), 0)
        zero = jnp.zeros((), jnp.float32)
        r_rows = jnp.where(
            rows16 == 0,
            r1.astype(jnp.float32),
            jnp.where(
                rows16 == 1,
                r2.astype(jnp.float32),
                jnp.where(rows16 == 2, r3.astype(jnp.float32), zero),
            ),
        ).astype(jnp.bfloat16)
        gram = lax.dot_general(c_near, every, dims, preferred_element_type=jnp.float32)
        v_rows = lax.dot_general(r_rows, every, dims, preferred_element_type=jnp.float32)
        v = jnp.sum(v_rows, axis=0, keepdims=True)
        grams.append((gram - v / n_all, total_sum(r * r)))
    per_view = tiles.shape[0] // 2
    for view, (gram, s) in enumerate(grams):
        for i in range(per_view):
            rt, lt = i // 2, i % 2
            tile = gram[rt * TILE_R : (rt + 1) * TILE_R, lt * TILE_C : (lt + 1) * TILE_C]
            if i == 0:
                tile = place(tile, 1, 0, s)
                if view == 0:
                    tile = place(tile, 3, 2, common)
            tiles[view * per_view + i] = tile


def final_kernel(n_all, f_all, tiles, cent_a, cent_b, base_a, base_b, grad_a, grad_b, part):
    n_dev = base_a.shape[0]
    coef = 2.0 * n_all / (25.0 * (n_all - 1))
    per_view = tiles.shape[0] // 2
    square = jnp.zeros((1, 1), jnp.float32)
    common = jnp.zeros((1, 1), jnp.float32)
    for view, (cent, base, grad) in enumerate(
        ((cent_a, base_a, grad_a), (cent_b, base_b, grad_b))
    ):
        rows = []
        for rt in range(per_view // 2):
            left, right = tiles[view * per_view + 2 * rt], tiles[view * per_view + 2 * rt + 1]
            rows.append(jnp.concatenate([left, right], axis=1))
        top = rows[0]
        s = pick(top, 1, 0)
        zero = jnp.float32(0.0)
        top = place(top, 1, 0, zero)
        if view == 0:
            common = common + pick(top, 3, 2)
            top = place(top, 3, 2, zero)
        sums = jnp.sum(top, axis=1, keepdims=True)

        def recover(row, col):
            delta = (sums[row : row + 1] - sums[col : col + 1]) / n_all
            return (pick(top, col, row) + delta) / (1.0 - 1.0 / n_all)

        fixed = place(top, 1, 0, recover(1, 0))
        if view == 0:
            fixed = place(fixed, 3, 2, recover(3, 2))
        rows[0] = fixed
        gram = jnp.concatenate(rows, axis=0)
        row_sums = jnp.sum(gram, axis=1, keepdims=True)
        square = square + total_sum(gram * gram) + total_sum(row_sums * row_sums) / n_all
        square = square + 0.5 * s * s / (n_all * n_all)
        parts = jnp.concatenate(split3(gram), axis=0)
        pulls = jnp.dot(parts, cent[...], preferred_element_type=jnp.float32)
        pull = pulls[:n_dev] + pulls[n_dev : 2 * n_dev] + pulls[2 * n_dev :]
        grad[...] = base[...] + (coef / (n_all - 1)) * pull
    loss = 0.5 * common + square / (float(n_all - 1) * float(n_all - 1) * f_all)
    part[...] = jnp.broadcast_to(loss * n_all / (50.0 * f_all), part.shape)


def on_device(view_a, view_b):
    n_dp = lax.axis_size("dp")
    n_chips = lax.axis_size(CHIPS)
    n_dev, shard = view_a.shape
    n_all = n_dev * n_dp
    f_all = shard * n_chips * lax.axis_size("core")
    swap = [(0, 1), (1, 0)]
    vmem = pl.BlockSpec(memory_space=pltpu.VMEM)
    far = lax.ppermute(jnp.stack([view_a, view_b]), "dp", swap)
    f32, bf16 = jnp.float32, jnp.bfloat16
    n_tiles = 2 * n_dev * n_all // (TILE_R * TILE_C)
    tiles, cent_a, cent_b, base_a, base_b = pl.pallas_call(
        lambda *refs: gram_kernel(n_all, f_all, *refs),
        out_shape=(
            jax.ShapeDtypeStruct((n_tiles, TILE_R, TILE_C), f32),
            jax.ShapeDtypeStruct((n_all, shard), bf16),
            jax.ShapeDtypeStruct((n_all, shard), bf16),
            jax.ShapeDtypeStruct((n_dev, shard), f32),
            jax.ShapeDtypeStruct((n_dev, shard), f32),
        ),
        in_specs=[vmem] * 3,
        out_specs=(vmem,) * 5,
        compiler_params=pltpu.CompilerParams(vmem_limit_bytes=32 * 1024 * 1024),
        name="gram",
    )(view_a, view_b, far)
    shares = lax.all_to_all(tiles, CHIPS, 0, 0, tiled=True)
    share = jnp.sum(shares.reshape(n_chips, n_tiles // n_chips, TILE_R, TILE_C), axis=0)
    share = share + lax.ppermute(share, "core", swap)
    spread = jnp.broadcast_to(share[None], (n_chips,) + share.shape)
    whole = lax.all_to_all(spread.reshape(tiles.shape), CHIPS, 0, 0, tiled=True)
    grad_a, grad_b, part = pl.pallas_call(
        lambda *refs: final_kernel(n_all, f_all, *refs),
        out_shape=(
            jax.ShapeDtypeStruct((n_dev, shard), f32),
            jax.ShapeDtypeStruct((n_dev, shard), f32),
            jax.ShapeDtypeStruct((TILE_R, TILE_C), f32),
        ),
        in_specs=[vmem] * 5,
        out_specs=(vmem,) * 3,
        compiler_params=pltpu.CompilerParams(vmem_limit_bytes=32 * 1024 * 1024),
        name="final",
    )(whole, cent_a, cent_b, base_a, base_b)
    objective = part[0, 0] + lax.ppermute(part, "dp", swap)[0, 0]
    return (grad_a, grad_b, objective)


def solution(mesh):
    fine = Mesh(mesh.devices.reshape(2, 4, 2, 8, 2), AXES)
    spec = P("dp", ("x", "yl", "z", "core"))
    return jax.shard_map(
        on_device, mesh=fine, in_specs=(spec, spec), out_specs=(spec, spec, P()), check_vma=False
    )
```

```python
import jax
import jax.numpy as jnp
from jax import lax
from jax.experimental import pallas as pl
from jax.experimental.pallas import tpu as pltpu
from jax.sharding import Mesh, PartitionSpec as P

AXES = ("dp", "x", "yl", "z", "core")
CHIPS = ("x", "yl", "z")
PIECES = 5
F32, BF16 = jnp.float32, jnp.bfloat16
ROW_DIMS = (((1,), (1,)), ((), ()))


def split3(value):
    first = value.astype(BF16)
    rest = value - first.astype(F32)
    second = rest.astype(BF16)
    third = (rest - second.astype(F32)).astype(BF16)
    return (first, second, third)


def iotas(shape):
    return (lax.broadcasted_iota(jnp.int32, shape, 0), lax.broadcasted_iota(jnp.int32, shape, 1))


def total_sum(value):
    return jnp.sum(value, axis=(0, 1), keepdims=True)


def col_sum(value):
    return jnp.sum(value, axis=0, keepdims=True)


def pack(gram, scalar):
    g00, g01, g11 = gram
    n = g00.shape[0]
    rows, cols = iotas(g00.shape)
    both = jnp.where(rows < cols, g00, g11)
    diag = col_sum(jnp.where(rows == cols, g00, F32(0.0)))
    erows, ecols = iotas((n // 2, n))
    extra = jnp.where(erows == 0, diag, F32(0.0))
    extra = jnp.where((erows == 1) & (ecols == 0), scalar, extra)
    return (both[: n // 2], both[n // 2 :], g01[: n // 2], g01[n // 2 :], extra)


def unpack(pieces):
    both = jnp.concatenate([pieces[0], pieces[1]], axis=0)
    g01 = jnp.concatenate([pieces[2], pieces[3]], axis=0)
    extra = pieces[4]
    rows, cols = iotas(both.shape)
    zero = F32(0.0)
    upper = jnp.where(rows < cols, both, zero)
    lower = jnp.where(rows > cols, both, zero)
    on_diag = rows == cols
    g00 = upper + upper.T + jnp.where(on_diag, extra[0:1], zero)
    g11 = lower + lower.T + jnp.where(on_diag, both, zero)
    return ((g00, g01, g11), extra[1:2, 0:1])


def store_pieces(ref, pieces):
    for j, piece in enumerate(pieces):
        ref[pl.ds(j, piece.shape[0], stride=PIECES), :] = piece


def load_pieces(ref):
    count = ref.shape[0] // PIECES
    return [ref[pl.ds(j, count, stride=PIECES), :] for j in range(PIECES)]


def gram_kernel(n_all, f_all, place, near, far, keep, send, cent, base):
    n_dev = near.shape[1]
    coef = 2.0 * n_all / (25.0 * (n_all - 1))
    first_plane = place[0] == 0
    first_core = place[1] == 0
    views = []
    for view in range(2):
        mine, theirs = near[view].astype(F32), far[view].astype(F32)
        views.append((jnp.where(first_plane, mine, theirs), jnp.where(first_plane, theirs, mine)))
    gap0 = views[0][0] - views[1][0]
    gap1 = views[0][1] - views[1][1]
    gap = jnp.where(first_plane, gap0, gap1)
    packed = []
    for view, (z0, z1) in enumerate(views):
        mean = (col_sum(z0) + col_sum(z1)) / n_all
        diff0, diff1 = z0 - mean, z1 - mean
        squares = col_sum(diff0 * diff0) + col_sum(diff1 * diff1)
        std = jnp.sqrt(squares / (n_all - 1) + 0.0001)
        c0, c1 = diff0.astype(BF16), diff1.astype(BF16)
        cent[view, :n_dev] = c0
        cent[view, n_dev:] = c1
        f0, f1 = c0.astype(F32), c1.astype(F32)
        r = col_sum(f0) + col_sum(f1)
        d = (col_sum(f0 * f0) + col_sum(f1 * f1)) / (n_all - 1)
        hinge = jnp.where(std < 1.0, n_all / (2.0 * std * (n_all - 1)), F32(0.0))
        diff = jnp.where(first_plane, diff0, diff1)
        own = jnp.where(first_plane, f0, f1)
        sign = 1.0 if view == 0 else -1.0
        base[view] = sign * gap - hinge * diff - coef * (d * (own - r / n_all))
        scalar = (25.0 / f_all) * total_sum(jnp.maximum(1.0 - std, 0.0)) - total_sum(d * d) / f_all
        if view == 0:
            squared_gap = total_sum(gap0 * gap0) + total_sum(gap1 * gap1)
            scalar = scalar + (25.0 / (n_all * f_all)) * squared_gap
        every = jnp.concatenate([c0, c1], axis=0)
        top = lax.dot_general(c0, every, ROW_DIMS, preferred_element_type=F32)
        low = lax.dot_general(c1, c1, ROW_DIMS, preferred_element_type=F32)
        packed.append(pack((top[:, :n_dev], top[:, n_dev:], low), scalar))
    store_pieces(keep, [jnp.where(first_core, a, b) for a, b in zip(*packed)])
    store_pieces(send, [jnp.where(first_core, b, a) for a, b in zip(*packed)])


def share_kernel(shares, spread):
    for j, piece in enumerate(load_pieces(shares)):
        spread[pl.ds(j, piece.shape[0], stride=PIECES), :] = jnp.broadcast_to(
            col_sum(piece), piece.shape
        )


def final_kernel(n_all, f_all, place, mine, theirs, cent, base, grad_a, grad_b, objective):
    n_dev = base.shape[1]
    coef = 2.0 * n_all / (25.0 * (n_all - 1))
    first_plane = place[0] == 0
    first_core = place[1] == 0
    mine_pieces, theirs_pieces = load_pieces(mine), load_pieces(theirs)
    square = jnp.zeros((1, 1), F32)
    loss = jnp.zeros((1, 1), F32)
    for view, grad in enumerate((grad_a, grad_b)):
        mine_here = first_core if view == 0 else jnp.logical_not(first_core)
        pieces = [jnp.where(mine_here, m, t) for m, t in zip(mine_pieces, theirs_pieces)]
        (g00, g01, g11), scalar = unpack(pieces)
        g10 = g01.T
        loss = loss + scalar
        square = square + total_sum(g00 * g00 + 2.0 * (g01 * g01) + g11 * g11)
        v0 = col_sum(g00) + col_sum(g10)
        v1 = col_sum(g01) + col_sum(g11)
        left = jnp.where(first_plane, g00, g10) - v0 / n_all
        right = jnp.where(first_plane, g01, g11) - v1 / n_all
        rows = jnp.concatenate([left, right], axis=1)
        parts = jnp.concatenate(split3(rows), axis=0)
        pulls = jnp.dot(parts, cent[view], preferred_element_type=F32)
        pull = pulls[:n_dev] + pulls[n_dev : 2 * n_dev] + pulls[2 * n_dev :]
        grad[...] = base[view] + (coef / (n_all - 1)) * pull
    loss = loss + square / (float(n_all - 1) * float(n_all - 1) * f_all)
    objective[...] = loss * n_all / (50.0 * f_all)


def on_device(view_a, view_b):
    n_dp = lax.axis_size("dp")
    n_chips = lax.axis_size(CHIPS)
    n_dev, shard = view_a.shape
    n_all = n_dev * n_dp
    f_all = shard * n_chips * lax.axis_size("core")
    swap = [(0, 1), (1, 0)]
    vmem = pl.BlockSpec(memory_space=pltpu.VMEM)
    smem = pl.BlockSpec(memory_space=pltpu.SMEM)
    params = pltpu.CompilerParams(vmem_limit_bytes=32 * 1024 * 1024)
    place = jnp.stack([lax.axis_index("dp"), lax.axis_index("core")]).astype(jnp.int32)
    near = jnp.stack([view_a, view_b])
    far = lax.ppermute(near, "dp", swap)
    half = n_dev // 2
    packed = jax.ShapeDtypeStruct((PIECES * half, n_dev), F32)
    keep, send, cent, base = pl.pallas_call(
        lambda *refs: gram_kernel(n_all, f_all, *refs),
        out_shape=(
            packed,
            packed,
            jax.ShapeDtypeStruct((2, n_all, shard), BF16),
            jax.ShapeDtypeStruct((2, n_dev, shard), F32),
        ),
        in_specs=[smem, vmem, vmem],
        out_specs=(vmem,) * 4,
        compiler_params=params,
        name="gram",
    )(place, near, far)

    def exchange(rows):
        chunks = rows.reshape(n_chips, 1, PIECES * half * n_dev // n_chips)
        moved = lax.all_to_all(chunks, CHIPS, 0, 0, tiled=True)
        return moved.reshape(rows.shape)

    chip_sum = keep + lax.ppermute(send, "core", swap)
    shares = exchange(chip_sum)
    spread = pl.pallas_call(
        share_kernel,
        out_shape=packed,
        in_specs=[vmem],
        out_specs=vmem,
        compiler_params=params,
        name="share",
    )(shares)
    mine = exchange(spread)
    theirs = lax.ppermute(mine, "core", swap)
    grad_a, grad_b, objective = pl.pallas_call(
        lambda *refs: final_kernel(n_all, f_all, *refs),
        out_shape=(
            jax.ShapeDtypeStruct((n_dev, shard), F32),
            jax.ShapeDtypeStruct((n_dev, shard), F32),
            jax.ShapeDtypeStruct((1, 1), F32),
        ),
        in_specs=[smem] + [vmem] * 4,
        out_specs=(vmem,) * 3,
        compiler_params=params,
        name="final",
    )(place, mine, theirs, cent, base)
    return (grad_a, grad_b, objective.reshape(()))


def solution(mesh):
    fine = Mesh(mesh.devices.reshape(2, 4, 2, 8, 2), AXES)
    spec = P("dp", ("x", "yl", "z", "core"))
    return jax.shard_map(
        on_device, mesh=fine, in_specs=(spec, spec), out_specs=(spec, spec, P()), check_vma=False
    )
```

```python
import jax
import jax.numpy as jnp
from jax import lax
from jax.experimental import pallas as pl
from jax.experimental.pallas import tpu as pltpu
from jax.sharding import Mesh, PartitionSpec as P

AXES = ("dp", "x", "yl", "z", "core")
SPLIT = ("x", "yl", "core")
RING = ("z",)
EXTRA = 16
F32, BF16 = jnp.float32, jnp.bfloat16
ROW_DIMS = (((1,), (1,)), ((), ()))


def split3(value):
    first = value.astype(BF16)
    rest = value - first.astype(F32)
    second = rest.astype(BF16)
    third = (rest - second.astype(F32)).astype(BF16)
    return (first, second, third)


def iotas(shape):
    return (lax.broadcasted_iota(jnp.int32, shape, 0), lax.broadcasted_iota(jnp.int32, shape, 1))


def total_sum(value):
    return jnp.sum(value, axis=(0, 1), keepdims=True)


def col_sum(value):
    return jnp.sum(value, axis=0, keepdims=True)


def pack(gram):
    g00, g01, g11 = gram
    rows, cols = iotas(g00.shape)
    both = jnp.where(rows < cols, g00, g11)
    diag = col_sum(jnp.where(rows == cols, g00, F32(0.0)))
    return (both, g01, diag)


def unpack(both, diag):
    rows, cols = iotas(both.shape)
    zero = F32(0.0)
    upper = jnp.where(rows < cols, both, zero)
    lower = jnp.where(rows > cols, both, zero)
    on_diag = rows == cols
    g00 = upper + upper.T + jnp.where(on_diag, diag, zero)
    g11 = lower + lower.T + jnp.where(on_diag, both, zero)
    return (g00, g11)


def gram_kernel(n_all, f_all, place, near, far, packed, cent, base):
    n_dev = near.shape[1]
    coef = 2.0 * n_all / (25.0 * (n_all - 1))
    first_plane = place[0] == 0
    views = []
    for view in range(2):
        mine, theirs = near[view].astype(F32), far[view].astype(F32)
        views.append((jnp.where(first_plane, mine, theirs), jnp.where(first_plane, theirs, mine)))
    gap0 = views[0][0] - views[1][0]
    gap1 = views[0][1] - views[1][1]
    gap = jnp.where(first_plane, gap0, gap1)
    loss = jnp.zeros((1, 1), F32)
    diags = []
    for view, (z0, z1) in enumerate(views):
        mean = (col_sum(z0) + col_sum(z1)) / n_all
        diff0, diff1 = z0 - mean, z1 - mean
        squares = col_sum(diff0 * diff0) + col_sum(diff1 * diff1)
        std = jnp.sqrt(squares / (n_all - 1) + 0.0001)
        c0, c1 = diff0.astype(BF16), diff1.astype(BF16)
        cent[view, :n_dev] = c0
        cent[view, n_dev:] = c1
        f0, f1 = c0.astype(F32), c1.astype(F32)
        r = col_sum(f0) + col_sum(f1)
        d = (col_sum(f0 * f0) + col_sum(f1 * f1)) / (n_all - 1)
        hinge = jnp.where(std < 1.0, n_all / (2.0 * std * (n_all - 1)), F32(0.0))
        diff = jnp.where(first_plane, diff0, diff1)
        own = jnp.where(first_plane, f0, f1)
        sign = 1.0 if view == 0 else -1.0
        base[view] = sign * gap - hinge * diff - coef * (d * (own - r / n_all))
        loss = loss + (25.0 / f_all) * total_sum(jnp.maximum(1.0 - std, 0.0))
        loss = loss - total_sum(d * d) / f_all
        every = jnp.concatenate([c0, c1], axis=0)
        top = lax.dot_general(c0, every, ROW_DIMS, preferred_element_type=F32)
        low = lax.dot_general(c1, c1, ROW_DIMS, preferred_element_type=F32)
        both, g01, diag = pack((top[:, :n_dev], top[:, n_dev:], low))
        packed[view * n_all : view * n_all + n_dev] = both
        packed[view * n_all + n_dev : (view + 1) * n_all] = g01
        diags.append(diag)
    squared_gap = total_sum(gap0 * gap0) + total_sum(gap1 * gap1)
    loss = loss + (25.0 / (n_all * f_all)) * squared_gap
    rows, unused = iotas((EXTRA, n_dev))
    extra = jnp.where(rows == 2, loss, F32(0.0))
    for view, diag in enumerate(diags):
        extra = jnp.where(rows == view, diag, extra)
    packed[2 * n_all :] = extra


def share_kernel(n_in, n_out, shares, spread):
    depth = shares.shape[0] // n_in
    total = shares[:depth]
    for i in range(1, n_in):
        total = total + shares[i * depth : (i + 1) * depth]
    for i in range(n_out):
        spread[i * depth : (i + 1) * depth] = total


def final_kernel(n_all, f_all, place, packed, cent, base, grad_a, grad_b, objective):
    n_dev = base.shape[1]
    coef = 2.0 * n_all / (25.0 * (n_all - 1))
    first_plane = place[0] == 0
    square = jnp.zeros((1, 1), F32)
    extra = packed[2 * n_all :]
    for view, grad in enumerate((grad_a, grad_b)):
        both = packed[view * n_all : view * n_all + n_dev]
        g01 = packed[view * n_all + n_dev : (view + 1) * n_all]
        g00, g11 = unpack(both, extra[view : view + 1])
        g10 = g01.T
        square = square + total_sum(g00 * g00 + 2.0 * (g01 * g01) + g11 * g11)
        v0 = col_sum(g00) + col_sum(g10)
        v1 = col_sum(g01) + col_sum(g11)
        left = jnp.where(first_plane, g00, g10) - v0 / n_all
        right = jnp.where(first_plane, g01, g11) - v1 / n_all
        rows = jnp.concatenate([left, right], axis=1)
        parts = jnp.concatenate(split3(rows), axis=0)
        pulls = jnp.dot(parts, cent[view], preferred_element_type=F32)
        pull = pulls[:n_dev] + pulls[n_dev : 2 * n_dev] + pulls[2 * n_dev :]
        grad[...] = base[view] + (coef / (n_all - 1)) * pull
    loss = extra[2:3, 0:1] + square / (float(n_all - 1) * float(n_all - 1) * f_all)
    objective[...] = loss * n_all / (50.0 * f_all)


def on_device(view_a, view_b):
    n_dp = lax.axis_size("dp")
    n_split, n_ring = lax.axis_size(SPLIT), lax.axis_size(RING)
    n_dev, shard = view_a.shape
    n_all = n_dev * n_dp
    f_all = shard * n_split * n_ring
    swap = [(0, 1), (1, 0)]
    vmem = pl.BlockSpec(memory_space=pltpu.VMEM)
    smem = pl.BlockSpec(memory_space=pltpu.SMEM)
    params = pltpu.CompilerParams(vmem_limit_bytes=32 * 1024 * 1024)
    place = lax.axis_index("dp").astype(jnp.int32).reshape(1)
    near = jnp.stack([view_a, view_b])
    far = lax.ppermute(near, "dp", swap)
    n_rows = 2 * n_all + EXTRA
    depth = n_rows // n_split
    packed, cent, base = pl.pallas_call(
        lambda *refs: gram_kernel(n_all, f_all, *refs),
        out_shape=(
            jax.ShapeDtypeStruct((n_rows, n_dev), F32),
            jax.ShapeDtypeStruct((2, n_all, shard), BF16),
            jax.ShapeDtypeStruct((2, n_dev, shard), F32),
        ),
        in_specs=[smem, vmem, vmem],
        out_specs=(vmem,) * 3,
        compiler_params=params,
        name="gram",
    )(place, near, far)

    def exchange(rows, axes):
        chunks = rows.reshape(lax.axis_size(axes), 1, depth * n_dev)
        return lax.all_to_all(chunks, axes, 0, 0, tiled=True).reshape(rows.shape)

    def share(rows, n_in, n_out):
        return pl.pallas_call(
            lambda *refs: share_kernel(n_in, n_out, *refs),
            out_shape=jax.ShapeDtypeStruct((n_out * depth, n_dev), F32),
            in_specs=[vmem],
            out_specs=vmem,
            compiler_params=params,
            name="share",
        )(rows)

    pieces = share(exchange(packed, SPLIT), n_split, n_ring)
    spread = share(exchange(pieces, RING), n_ring, n_split)
    whole = exchange(spread, SPLIT)
    grad_a, grad_b, objective = pl.pallas_call(
        lambda *refs: final_kernel(n_all, f_all, *refs),
        out_shape=(
            jax.ShapeDtypeStruct((n_dev, shard), F32),
            jax.ShapeDtypeStruct((n_dev, shard), F32),
            jax.ShapeDtypeStruct((1, 1), F32),
        ),
        in_specs=[smem] + [vmem] * 3,
        out_specs=(vmem,) * 3,
        compiler_params=params,
        name="final",
    )(place, whole, cent, base)
    return (grad_a, grad_b, objective.reshape(()))


def solution(mesh):
    fine = Mesh(mesh.devices.reshape(2, 4, 2, 8, 2), AXES)
    spec = P("dp", ("x", "yl", "z", "core"))
    return jax.shard_map(
        on_device, mesh=fine, in_specs=(spec, spec), out_specs=(spec, spec, P()), check_vma=False
    )
```

```python
import jax
import jax.numpy as jnp
from jax import lax
from jax.experimental import pallas as pl
from jax.experimental.pallas import tpu as pltpu
from jax.sharding import Mesh, PartitionSpec as P

N_X, N_Y, N_Z, N_CORE = 4, 2, 8, 2
RING_ORDER = (4, 0, 1, 2, 3, 5, 6, 7)
SPLIT_ORDER = ((2, 1, 1), (2, 1, 0), (3, 1, 1), (1, 1, 1), (0, 1, 1), (3, 0, 1), (2, 0, 1), (1, 0, 1), (0, 0, 1), (3, 1, 0), (1, 1, 0), (0, 1, 0), (3, 0, 0), (2, 0, 0), (1, 0, 0), (0, 0, 0))


def place_of(x, y, z, core):
    return ((x * N_Y + y) * N_Z + z) * N_CORE + core


SPLIT = [[place_of(x, y, z, c) for x, y, c in SPLIT_ORDER] for z in range(N_Z)]
RING = [[place_of(x, y, z, c) for z in RING_ORDER] for x, y, c in SPLIT_ORDER]
EXTRA = 16
F32, BF16 = jnp.float32, jnp.bfloat16
ROW_DIMS = (((1,), (1,)), ((), ()))


def split3(value):
    first = value.astype(BF16)
    rest = value - first.astype(F32)
    second = rest.astype(BF16)
    third = (rest - second.astype(F32)).astype(BF16)
    return (first, second, third)


def iotas(shape):
    return (lax.broadcasted_iota(jnp.int32, shape, 0), lax.broadcasted_iota(jnp.int32, shape, 1))


def total_sum(value):
    return jnp.sum(value, axis=(0, 1), keepdims=True)


def col_sum(value):
    return jnp.sum(value, axis=0, keepdims=True)


def pack(gram):
    g00, g01, g11 = gram
    rows, cols = iotas(g00.shape)
    both = jnp.where(rows < cols, g00, g11)
    diag = col_sum(jnp.where(rows == cols, g00, F32(0.0)))
    return (both, g01, diag)


def gram_kernel(n_all, f_all, place, near, far, packed, cent, base):
    @pl.when(place[0] == 0)
    def _():
        gram_body(n_all, f_all, (near, far), 0, packed, cent, base)

    @pl.when(place[0] != 0)
    def _():
        gram_body(n_all, f_all, (far, near), 1, packed, cent, base)


def gram_body(n_all, f_all, halves, plane, packed, cent, base):
    n_dev = halves[0].shape[1]
    coef = 2.0 * n_all / (25.0 * (n_all - 1))
    views = [[half[view].astype(F32) for half in halves] for view in range(2)]
    gaps = [views[0][i] - views[1][i] for i in range(2)]
    loss = jnp.zeros((1, 1), F32)
    diags = []
    for view, zs in enumerate(views):
        mean = (col_sum(zs[0]) + col_sum(zs[1])) / n_all
        diffs = [z - mean for z in zs]
        squares = col_sum(diffs[0] * diffs[0] + diffs[1] * diffs[1])
        std = jnp.sqrt(squares / (n_all - 1) + 0.0001)
        cs = [diff.astype(BF16) for diff in diffs]
        cent[view, :n_dev] = cs[0]
        cent[view, n_dev:] = cs[1]
        every = jnp.concatenate(cs, axis=0)
        top = lax.dot_general(cs[0], every, ROW_DIMS, preferred_element_type=F32)
        low = lax.dot_general(cs[1], cs[1], ROW_DIMS, preferred_element_type=F32)
        fs = [c.astype(F32) for c in cs]
        r = col_sum(fs[0] + fs[1])
        d = col_sum(fs[0] * fs[0] + fs[1] * fs[1]) / (n_all - 1)
        hinge = jnp.where(std < 1.0, n_all / (2.0 * std * (n_all - 1)), F32(0.0))
        pulled = coef * d
        rest = gaps[plane] if view == 0 else -gaps[plane]
        base[view] = rest - hinge * diffs[plane] - pulled * fs[plane] + pulled * (r / n_all)
        terms = 25.0 * jnp.maximum(1.0 - std, 0.0) - d * d
        loss = loss + total_sum(terms) / f_all
        both, g01, diag = pack((top[:, :n_dev], top[:, n_dev:], low))
        packed[view * n_all : view * n_all + n_dev] = both
        packed[view * n_all + n_dev : (view + 1) * n_all] = g01
        diags.append(diag)
    squared_gap = total_sum(gaps[0] * gaps[0] + gaps[1] * gaps[1])
    loss = loss + (25.0 / (n_all * f_all)) * squared_gap
    rows, unused = iotas((EXTRA, n_dev))
    extra = jnp.where(rows == 2, loss, F32(0.0))
    for view, diag in enumerate(diags):
        extra = jnp.where(rows == view, diag, extra)
    packed[2 * n_all :] = extra


def share_kernel(n_in, n_out, shares, spread):
    depth = shares.shape[0] // n_in
    total = shares[:depth]
    for i in range(1, n_in):
        total = total + shares[i * depth : (i + 1) * depth]
    for i in range(n_out):
        spread[i * depth : (i + 1) * depth] = total


def final_kernel(n_all, f_all, place, packed, cent, base, grad_a, grad_b, objective):
    n_dev = base.shape[1]
    coef = 2.0 * n_all / (25.0 * (n_all - 1))
    first_plane = place[0] == 0
    rows, cols = iotas((n_dev, n_dev))
    on_diag, above = rows == cols, rows < cols
    zero = F32(0.0)
    square = jnp.zeros((1, 1), F32)
    extra = packed[2 * n_all :]
    for view, grad in enumerate((grad_a, grad_b)):
        both = packed[view * n_all : view * n_all + n_dev]
        g01 = packed[view * n_all + n_dev : (view + 1) * n_all]
        diag0 = extra[view : view + 1]
        diag1 = col_sum(jnp.where(on_diag, both, zero))
        square = square + 2.0 * total_sum(both * both + g01 * g01)
        square = square + total_sum(diag0 * diag0 - diag1 * diag1)
        turned, g10 = both.T, g01.T
        g00 = jnp.where(above, both, jnp.where(on_diag, diag0, turned))
        g11 = jnp.where(above, turned, both)
        v0 = col_sum(g00 + g10) / n_all
        v1 = col_sum(g01 + g11) / n_all
        left = jnp.where(first_plane, g00, g10) - v0
        right = jnp.where(first_plane, g01, g11) - v1
        parts = jnp.concatenate(split3(jnp.concatenate([left, right], axis=1)), axis=0)
        pulls = jnp.dot(parts, cent[view], preferred_element_type=F32)
        pull = pulls[:n_dev] + pulls[n_dev : 2 * n_dev] + pulls[2 * n_dev :]
        grad[...] = base[view] + (coef / (n_all - 1)) * pull
    loss = extra[2:3, 0:1] + square / (float(n_all - 1) * float(n_all - 1) * f_all)
    objective[...] = loss * n_all / (50.0 * f_all)


def on_device(view_a, view_b):
    n_dp = lax.axis_size("dp")
    n_split, n_ring = len(SPLIT_ORDER), len(RING_ORDER)
    n_dev, shard = view_a.shape
    n_all = n_dev * n_dp
    f_all = shard * n_split * n_ring
    swap = [(0, 1), (1, 0)]
    vmem = pl.BlockSpec(memory_space=pltpu.VMEM)
    smem = pl.BlockSpec(memory_space=pltpu.SMEM)
    params = pltpu.CompilerParams(vmem_limit_bytes=32 * 1024 * 1024)
    place = lax.axis_index("dp").astype(jnp.int32).reshape(1)
    near = jnp.stack([view_a, view_b])
    far = lax.ppermute(near, "dp", swap)
    n_rows = 2 * n_all + EXTRA
    depth = n_rows // n_split
    packed, cent, base = pl.pallas_call(
        lambda *refs: gram_kernel(n_all, f_all, *refs),
        out_shape=(
            jax.ShapeDtypeStruct((n_rows, n_dev), F32),
            jax.ShapeDtypeStruct((2, n_all, shard), BF16),
            jax.ShapeDtypeStruct((2, n_dev, shard), F32),
        ),
        in_specs=[smem, vmem, vmem],
        out_specs=(vmem,) * 3,
        compiler_params=params,
        name="gram",
    )(place, near, far)

    def exchange(rows, groups):
        chunks = rows.reshape(len(groups[0]), 1, depth * n_dev)
        moved = lax.all_to_all(chunks, "f", 0, 0, axis_index_groups=groups, tiled=True)
        return moved.reshape(rows.shape)

    def share(rows, n_in, n_out):
        return pl.pallas_call(
            lambda *refs: share_kernel(n_in, n_out, *refs),
            out_shape=jax.ShapeDtypeStruct((n_out * depth, n_dev), F32),
            in_specs=[vmem],
            out_specs=vmem,
            compiler_params=params,
            name="share",
        )(rows)

    pieces = share(exchange(packed, SPLIT), n_split, n_ring)
    spread = share(exchange(pieces, RING), n_ring, n_split)
    whole = exchange(spread, SPLIT)
    grad_a, grad_b, objective = pl.pallas_call(
        lambda *refs: final_kernel(n_all, f_all, *refs),
        out_shape=(
            jax.ShapeDtypeStruct((n_dev, shard), F32),
            jax.ShapeDtypeStruct((n_dev, shard), F32),
            jax.ShapeDtypeStruct((1, 1), F32),
        ),
        in_specs=[smem] + [vmem] * 3,
        out_specs=(vmem,) * 3,
        compiler_params=params,
        name="final",
    )(place, whole, cent, base)
    return (grad_a, grad_b, objective.reshape(()))


def solution(mesh):
    n_dp, n_row, n_col = (mesh.shape[name] for name in ("dp", "row", "col"))
    flat = Mesh(mesh.devices.reshape(n_dp, n_row * n_col), ("dp", "f"))
    spec = P("dp", "f")
    return jax.shard_map(
        on_device, mesh=flat, in_specs=(spec, spec), out_specs=(spec, spec, P()), check_vma=False
    )
```

```python
import jax
import jax.numpy as jnp
from jax import lax
from jax.experimental import pallas as pl
from jax.experimental.pallas import tpu as pltpu
from jax.sharding import Mesh, PartitionSpec as P

N_X, N_Y, N_Z, N_CORE = 4, 2, 8, 2
RING_ORDER = (5, 6, 3, 2, 1, 0, 4, 7)
SPLIT_ORDER = ((2, 1, 1), (0, 1, 0), (1, 1, 0), (3, 1, 0), (2, 0, 0), (2, 1, 0), (1, 0, 0), (3, 0, 0), (0, 0, 0), (1, 1, 1), (3, 1, 1), (1, 0, 1), (0, 1, 1), (2, 0, 1), (3, 0, 1), (0, 0, 1))


def place_of(x, y, z, core):
    return ((x * N_Y + y) * N_Z + z) * N_CORE + core


SPLIT = [[place_of(x, y, z, c) for x, y, c in SPLIT_ORDER] for z in range(N_Z)]
RING = [[place_of(x, y, z, c) for z in RING_ORDER] for x, y, c in SPLIT_ORDER]
FOLD, CROSS = 4, 8
PER_VIEW = 2 * FOLD + CROSS
DEPTH = 2 * PER_VIEW + 1
OUT_VIEW = FOLD + CROSS
OUT_DEPTH = 2 * OUT_VIEW + 2
F32, BF16 = jnp.float32, jnp.bfloat16
ROW_DIMS = (((1,), (1,)), ((), ()))


def split3(value):
    first = value.astype(BF16)
    rest = value - first.astype(F32)
    second = rest.astype(BF16)
    third = (rest - second.astype(F32)).astype(BF16)
    return (first, second, third)


def iotas(shape):
    return (lax.broadcasted_iota(jnp.int32, shape, 0), lax.broadcasted_iota(jnp.int32, shape, 1))


def total_sum(value):
    return jnp.sum(value, axis=(0, 1), keepdims=True)


def col_sum(value):
    return jnp.sum(value, axis=0, keepdims=True)


def roll_half(value):
    return pltpu.roll(value, value.shape[1] // 2, 1)


def fold(gram):
    half = gram.shape[0] // 2
    top, low = gram[:half], roll_half(gram[half:])
    rows, cols = iotas(top.shape)
    return jnp.where(rows < cols, top, low)


def unfold(folded, diag):
    square = jnp.concatenate([folded, roll_half(folded)], axis=0)
    turned = square.T
    rows, cols = iotas(square.shape)
    half = square.shape[0] // 2
    first = jnp.where(rows < cols, square, jnp.where(rows == cols, diag, turned))
    second = jnp.where(rows < cols, turned, square)
    return jnp.where((rows >= half) & (cols >= half), second, first)


def put_rows(ref, depth, start, value):
    chunks = ref.shape[0] // depth
    for j in range(value.shape[0] // chunks):
        ref[pl.ds(start + j, chunks, stride=depth), :] = value[j * chunks : (j + 1) * chunks]


def take_rows(ref, depth, start, count):
    chunks = ref.shape[0] // depth
    parts = [ref[pl.ds(start + j, chunks, stride=depth), :] for j in range(count)]
    return jnp.concatenate(parts, axis=0)


def gram_kernel(n_all, f_all, place, near, far, packed, cent, base):
    @pl.when(place[0] == 0)
    def _():
        gram_body(n_all, f_all, (near, far), 0, packed, cent, base)

    @pl.when(place[0] != 0)
    def _():
        gram_body(n_all, f_all, (far, near), 1, packed, cent, base)


def gram_body(n_all, f_all, halves, plane, packed, cent, base):
    n_dev = halves[0].shape[1]
    coef = 2.0 * n_all / (25.0 * (n_all - 1))
    views = [[half[view].astype(F32) for half in halves] for view in range(2)]
    gaps = [views[0][i] - views[1][i] for i in range(2)]
    loss = jnp.zeros((1, 1), F32)
    lines = []
    for view, zs in enumerate(views):
        mean = (col_sum(zs[0]) + col_sum(zs[1])) / n_all
        diffs = [z - mean for z in zs]
        squares = col_sum(diffs[0] * diffs[0] + diffs[1] * diffs[1])
        std = jnp.sqrt(squares / (n_all - 1) + 0.0001)
        cs = [diff.astype(BF16) for diff in diffs]
        cent[view, :n_dev] = cs[0]
        cent[view, n_dev:] = cs[1]
        every = jnp.concatenate(cs, axis=0)
        top = lax.dot_general(cs[0], every, ROW_DIMS, preferred_element_type=F32)
        low = lax.dot_general(cs[1], cs[1], ROW_DIMS, preferred_element_type=F32)
        fs = [c.astype(F32) for c in cs]
        r = col_sum(fs[0] + fs[1])
        d = col_sum(fs[0] * fs[0] + fs[1] * fs[1]) / (n_all - 1)
        hinge = jnp.where(std < 1.0, n_all / (2.0 * std * (n_all - 1)), F32(0.0))
        pulled = coef * d
        rest = gaps[plane] if view == 0 else -gaps[plane]
        base[view] = rest - hinge * diffs[plane] - pulled * fs[plane] + pulled * (r / n_all)
        terms = 25.0 * jnp.maximum(1.0 - std, 0.0) - d * d
        loss = loss + total_sum(terms) / f_all
        g00, g01 = top[:, :n_dev], top[:, n_dev:]
        put_rows(packed, DEPTH, view * PER_VIEW, fold(g00))
        put_rows(packed, DEPTH, view * PER_VIEW + FOLD, fold(low))
        put_rows(packed, DEPTH, view * PER_VIEW + 2 * FOLD, g01)
        rows, cols = iotas(g00.shape)
        for block in (g00, low):
            lines.append(col_sum(jnp.where(rows == cols, block, F32(0.0))))
            lines.append(col_sum(block))
    squared_gap = total_sum(gaps[0] * gaps[0] + gaps[1] * gaps[1])
    loss = loss + (25.0 / (n_all * f_all)) * squared_gap
    rows, unused = iotas((packed.shape[0] // DEPTH, n_dev))
    extra = jnp.where(rows == len(lines), loss, F32(0.0))
    for i, line in enumerate(lines):
        extra = jnp.where(rows == i, line, extra)
    put_rows(packed, DEPTH, DEPTH - 1, extra)


def chunk_sum(shares):
    total = shares[:DEPTH]
    for i in range(1, shares.shape[0] // DEPTH):
        total = total + shares[i * DEPTH : (i + 1) * DEPTH]
    return total


def share_kernel(shares, spread):
    total = chunk_sum(shares)
    for i in range(spread.shape[0] // DEPTH):
        spread[i * DEPTH : (i + 1) * DEPTH] = total


def spread_kernel(place, shares, spread):
    total = chunk_sum(shares)
    first_plane = place[0] == 0
    pieces = []
    for view in range(2):
        start = view * PER_VIEW
        block0, block1 = total[start : start + FOLD], total[start + FOLD : start + 2 * FOLD]
        pieces.append(jnp.where(first_plane, block0, block1))
        pieces.append(total[start + 2 * FOLD : start + PER_VIEW])
    pieces.append(total[DEPTH - 1 :])
    body = total[: DEPTH - 1]
    pieces.append(jnp.broadcast_to(2.0 * total_sum(body * body), (1, total.shape[1])))
    chunk = jnp.concatenate(pieces, axis=0)
    for i in range(spread.shape[0] // OUT_DEPTH):
        spread[i * OUT_DEPTH : (i + 1) * OUT_DEPTH] = chunk


def final_kernel(n_all, f_all, place, packed, cent, base, grad_a, grad_b, objective):
    n_dev = base.shape[1]
    coef = 2.0 * n_all / (25.0 * (n_all - 1))
    first_plane = place[0] == 0
    extra = take_rows(packed, OUT_DEPTH, OUT_DEPTH - 2, 1)
    norms = take_rows(packed, OUT_DEPTH, OUT_DEPTH - 1, 1)
    square = jnp.sum(norms[:, 0:1], axis=0, keepdims=True)
    unused, lanes = iotas((1, n_dev))
    for view, grad in enumerate((grad_a, grad_b)):
        folded = take_rows(packed, OUT_DEPTH, view * OUT_VIEW, FOLD)
        g01 = take_rows(packed, OUT_DEPTH, view * OUT_VIEW + FOLD, CROSS)
        diag0, sum0, diag1, sum1 = (extra[4 * view + i : 4 * view + i + 1] for i in range(4))
        diags = diag0 * diag0 + diag1 * diag1
        square = square + total_sum(jnp.where(lanes < n_dev // 2, diags, -diags))
        block = unfold(folded, jnp.where(first_plane, diag0, diag1))
        g10 = g01.T
        v0 = (sum0 + col_sum(g10)) / n_all
        v1 = (sum1 + col_sum(g01)) / n_all
        left = jnp.where(first_plane, block, g10) - v0
        right = jnp.where(first_plane, g01, block) - v1
        parts = jnp.concatenate(split3(jnp.concatenate([left, right], axis=1)), axis=0)
        pulls = jnp.dot(parts, cent[view], preferred_element_type=F32)
        pull = pulls[:n_dev] + pulls[n_dev : 2 * n_dev] + pulls[2 * n_dev :]
        grad[...] = base[view] + (coef / (n_all - 1)) * pull
    loss = extra[8:9, 0:1] + square / (float(n_all - 1) * float(n_all - 1) * f_all)
    objective[...] = loss * n_all / (50.0 * f_all)


def on_device(view_a, view_b):
    n_dp = lax.axis_size("dp")
    n_split, n_ring = len(SPLIT_ORDER), len(RING_ORDER)
    n_dev, shard = view_a.shape
    n_all = n_dev * n_dp
    f_all = shard * n_split * n_ring
    swap = [(0, 1), (1, 0)]
    vmem = pl.BlockSpec(memory_space=pltpu.VMEM)
    smem = pl.BlockSpec(memory_space=pltpu.SMEM)
    params = pltpu.CompilerParams(vmem_limit_bytes=32 * 1024 * 1024)
    place = lax.axis_index("dp").astype(jnp.int32).reshape(1)
    near = jnp.stack([view_a, view_b])
    far = lax.ppermute(near, "dp", swap)
    n_rows = n_split * DEPTH
    packed, cent, base = pl.pallas_call(
        lambda *refs: gram_kernel(n_all, f_all, *refs),
        out_shape=(
            jax.ShapeDtypeStruct((n_rows, n_dev), F32),
            jax.ShapeDtypeStruct((2, n_all, shard), BF16),
            jax.ShapeDtypeStruct((2, n_dev, shard), F32),
        ),
        in_specs=[smem, vmem, vmem],
        out_specs=(vmem,) * 3,
        compiler_params=params,
        name="gram",
    )(place, near, far)

    def exchange(rows, groups):
        count = len(groups[0])
        chunks = rows.reshape(count, 1, rows.shape[0] // count * n_dev)
        moved = lax.all_to_all(chunks, "f", 0, 0, axis_index_groups=groups, tiled=True)
        return moved.reshape(rows.shape)

    shares = exchange(packed, SPLIT)
    pieces = pl.pallas_call(
        share_kernel,
        out_shape=jax.ShapeDtypeStruct((n_ring * DEPTH, n_dev), F32),
        in_specs=[vmem],
        out_specs=vmem,
        compiler_params=params,
        name="share",
    )(shares)
    spread = pl.pallas_call(
        spread_kernel,
        out_shape=jax.ShapeDtypeStruct((n_split * OUT_DEPTH, n_dev), F32),
        in_specs=[smem, vmem],
        out_specs=vmem,
        compiler_params=params,
        name="spread",
    )(place, exchange(pieces, RING))
    whole = exchange(spread, SPLIT)
    grad_a, grad_b, objective = pl.pallas_call(
        lambda *refs: final_kernel(n_all, f_all, *refs),
        out_shape=(
            jax.ShapeDtypeStruct((n_dev, shard), F32),
            jax.ShapeDtypeStruct((n_dev, shard), F32),
            jax.ShapeDtypeStruct((1, 1), F32),
        ),
        in_specs=[smem] + [vmem] * 3,
        out_specs=(vmem,) * 3,
        compiler_params=params,
        name="final",
    )(place, whole, cent, base)
    return (grad_a, grad_b, objective.reshape(()))


def solution(mesh):
    n_dp, n_row, n_col = (mesh.shape[name] for name in ("dp", "row", "col"))
    flat = Mesh(mesh.devices.reshape(n_dp, n_row * n_col), ("dp", "f"))
    spec = P("dp", "f")
    return jax.shard_map(
        on_device, mesh=flat, in_specs=(spec, spec), out_specs=(spec, spec, P()), check_vma=False
    )
```

```python
import jax
import jax.numpy as jnp
from jax import lax
from jax.experimental import pallas as pl
from jax.experimental.pallas import tpu as pltpu
from jax.sharding import Mesh, PartitionSpec as P

N_X, N_Y, N_Z, N_CORE = 4, 2, 8, 2
RING_ORDER = (5, 6, 3, 2, 1, 0, 4, 7)
SPLIT_ORDER = ((2, 1, 1), (3, 1, 1), (2, 1, 0), (2, 0, 1), (1, 1, 1), (2, 0, 0), (3, 1, 0), (1, 1, 0), (0, 0, 1), (3, 0, 1), (3, 0, 0), (1, 0, 1), (1, 0, 0), (0, 0, 0), (0, 1, 1), (0, 1, 0))


def place_of(x, y, z, core):
    return ((x * N_Y + y) * N_Z + z) * N_CORE + core


SPLIT = [[place_of(x, y, z, c) for x, y, c in SPLIT_ORDER] for z in range(N_Z)]
RING = [[place_of(x, y, z, c) for z in RING_ORDER] for x, y, c in SPLIT_ORDER]
FOLD, CROSS = 4, 8
PER_VIEW = 2 * FOLD + CROSS
DEPTH = 2 * PER_VIEW + 1
OUT_VIEW = FOLD + CROSS
OUT_DEPTH = 2 * OUT_VIEW + 2
F32, BF16 = jnp.float32, jnp.bfloat16
ROW_DIMS = (((1,), (1,)), ((), ()))


def split3(value):
    first = value.astype(BF16)
    rest = value - first.astype(F32)
    second = rest.astype(BF16)
    third = (rest - second.astype(F32)).astype(BF16)
    return (first, second, third)


def iotas(shape):
    return (lax.broadcasted_iota(jnp.int32, shape, 0), lax.broadcasted_iota(jnp.int32, shape, 1))


def total_sum(value):
    return jnp.sum(value, axis=(0, 1), keepdims=True)


def col_sum(value):
    return jnp.sum(value, axis=0, keepdims=True)


def roll_half(value):
    return pltpu.roll(value, value.shape[1] // 2, 1)


def fold(gram):
    half = gram.shape[0] // 2
    top, low = gram[:half], roll_half(gram[half:])
    rows, cols = iotas(top.shape)
    return jnp.where(rows < cols, top, low)


def unfold(folded, diag):
    square = jnp.concatenate([folded, roll_half(folded)], axis=0)
    turned = square.T
    rows, cols = iotas(square.shape)
    half = square.shape[0] // 2
    first = jnp.where(rows < cols, square, jnp.where(rows == cols, diag, turned))
    second = jnp.where(rows < cols, turned, square)
    return jnp.where((rows >= half) & (cols >= half), second, first)


def put_rows(ref, depth, start, value):
    chunks = ref.shape[0] // depth
    for j in range(value.shape[0] // chunks):
        ref[pl.ds(start + j, chunks, stride=depth), :] = value[j * chunks : (j + 1) * chunks]


def take_rows(ref, depth, start, count):
    chunks = ref.shape[0] // depth
    parts = [ref[pl.ds(start + j, chunks, stride=depth), :] for j in range(count)]
    return jnp.concatenate(parts, axis=0)


def gram_kernel(n_all, f_all, place, near, far, packed, cent, base):
    @pl.when(place[0] == 0)
    def _():
        gram_body(n_all, f_all, (near, far), 0, packed, cent, base)

    @pl.when(place[0] != 0)
    def _():
        gram_body(n_all, f_all, (far, near), 1, packed, cent, base)


def gram_body(n_all, f_all, halves, plane, packed, cent, base):
    n_dev = halves[0].shape[1]
    coef = 2.0 * n_all / (25.0 * (n_all - 1))
    views = [[half[view].astype(F32) for half in halves] for view in range(2)]
    gaps = [views[0][i] - views[1][i] for i in range(2)]
    loss = jnp.zeros((1, 1), F32)
    lines = []
    for view, zs in enumerate(views):
        mean = (col_sum(zs[0]) + col_sum(zs[1])) / n_all
        diffs = [z - mean for z in zs]
        squares = col_sum(diffs[0] * diffs[0] + diffs[1] * diffs[1])
        std = jnp.sqrt(squares / (n_all - 1) + 0.0001)
        cs = [diff.astype(BF16) for diff in diffs]
        cent[view, :n_dev] = cs[0]
        cent[view, n_dev:] = cs[1]
        every = jnp.concatenate(cs, axis=0)
        top = lax.dot_general(cs[0], every, ROW_DIMS, preferred_element_type=F32)
        low = lax.dot_general(cs[1], cs[1], ROW_DIMS, preferred_element_type=F32)
        fs = [c.astype(F32) for c in cs]
        r = col_sum(fs[0] + fs[1])
        d = col_sum(fs[0] * fs[0] + fs[1] * fs[1]) / (n_all - 1)
        hinge = jnp.where(std < 1.0, n_all / (2.0 * std * (n_all - 1)), F32(0.0))
        pulled = coef * d
        rest = gaps[plane] if view == 0 else -gaps[plane]
        base[view] = rest - hinge * diffs[plane] - pulled * fs[plane] + pulled * (r / n_all)
        terms = 25.0 * jnp.maximum(1.0 - std, 0.0) - d * d
        loss = loss + total_sum(terms) / f_all
        g00, g01 = top[:, :n_dev], top[:, n_dev:]
        put_rows(packed, DEPTH, view * PER_VIEW, fold(g00))
        put_rows(packed, DEPTH, view * PER_VIEW + FOLD, fold(low))
        put_rows(packed, DEPTH, view * PER_VIEW + 2 * FOLD, g01)
        rows, cols = iotas(g00.shape)
        for block in (g00, low):
            lines.append(col_sum(jnp.where(rows == cols, block, F32(0.0))))
            lines.append(col_sum(block))
    squared_gap = total_sum(gaps[0] * gaps[0] + gaps[1] * gaps[1])
    loss = loss + (25.0 / (n_all * f_all)) * squared_gap
    rows, unused = iotas((packed.shape[0] // DEPTH, n_dev))
    extra = jnp.where(rows == len(lines), loss, F32(0.0))
    for i, line in enumerate(lines):
        extra = jnp.where(rows == i, line, extra)
    put_rows(packed, DEPTH, DEPTH - 1, extra)


def chunk_sum(shares):
    total = shares[:DEPTH]
    for i in range(1, shares.shape[0] // DEPTH):
        total = total + shares[i * DEPTH : (i + 1) * DEPTH]
    return total


def share_kernel(shares, spread):
    total = chunk_sum(shares)
    for i in range(spread.shape[0] // DEPTH):
        spread[i * DEPTH : (i + 1) * DEPTH] = total


def spread_kernel(place, shares, spread):
    total = chunk_sum(shares)
    first_plane = place[0] == 0
    pieces = []
    for view in range(2):
        start = view * PER_VIEW
        block0, block1 = total[start : start + FOLD], total[start + FOLD : start + 2 * FOLD]
        pieces.append(jnp.where(first_plane, block0, block1))
        pieces.append(total[start + 2 * FOLD : start + PER_VIEW])
    pieces.append(total[DEPTH - 1 :])
    body = total[: DEPTH - 1]
    pieces.append(jnp.broadcast_to(2.0 * total_sum(body * body), (1, total.shape[1])))
    chunk = jnp.concatenate(pieces, axis=0)
    for i in range(spread.shape[0] // OUT_DEPTH):
        spread[i * OUT_DEPTH : (i + 1) * OUT_DEPTH] = chunk


def final_kernel(n_all, f_all, place, packed, cent, base, grad_a, grad_b, objective):
    n_dev = base.shape[1]
    coef = 2.0 * n_all / (25.0 * (n_all - 1))
    first_plane = place[0] == 0
    extra = take_rows(packed, OUT_DEPTH, OUT_DEPTH - 2, 1)
    norms = take_rows(packed, OUT_DEPTH, OUT_DEPTH - 1, 1)
    square = jnp.sum(norms[:, 0:1], axis=0, keepdims=True)
    unused, lanes = iotas((1, n_dev))
    for view, grad in enumerate((grad_a, grad_b)):
        folded = take_rows(packed, OUT_DEPTH, view * OUT_VIEW, FOLD)
        g01 = take_rows(packed, OUT_DEPTH, view * OUT_VIEW + FOLD, CROSS)
        diag0, sum0, diag1, sum1 = (extra[4 * view + i : 4 * view + i + 1] for i in range(4))
        diags = diag0 * diag0 + diag1 * diag1
        square = square + total_sum(jnp.where(lanes < n_dev // 2, diags, -diags))
        block = unfold(folded, jnp.where(first_plane, diag0, diag1))
        g10 = g01.T
        v0 = (sum0 + col_sum(g10)) / n_all
        v1 = (sum1 + col_sum(g01)) / n_all
        left = jnp.where(first_plane, block, g10) - v0
        right = jnp.where(first_plane, g01, block) - v1
        parts = jnp.concatenate(split3(jnp.concatenate([left, right], axis=1)), axis=0)
        pulls = jnp.dot(parts, cent[view], preferred_element_type=F32)
        pull = pulls[:n_dev] + pulls[n_dev : 2 * n_dev] + pulls[2 * n_dev :]
        grad[...] = base[view] + (coef / (n_all - 1)) * pull
    loss = extra[8:9, 0:1] + square / (float(n_all - 1) * float(n_all - 1) * f_all)
    objective[...] = loss * n_all / (50.0 * f_all)


def on_device(view_a, view_b):
    n_dp = lax.axis_size("dp")
    n_split, n_ring = len(SPLIT_ORDER), len(RING_ORDER)
    n_dev, shard = view_a.shape
    n_all = n_dev * n_dp
    f_all = shard * n_split * n_ring
    swap = [(0, 1), (1, 0)]
    vmem = pl.BlockSpec(memory_space=pltpu.VMEM)
    smem = pl.BlockSpec(memory_space=pltpu.SMEM)
    params = pltpu.CompilerParams(vmem_limit_bytes=32 * 1024 * 1024)
    place = lax.axis_index("dp").astype(jnp.int32).reshape(1)
    near = jnp.stack([view_a, view_b])
    far = lax.ppermute(near, "dp", swap)
    n_rows = n_split * DEPTH
    packed, cent, base = pl.pallas_call(
        lambda *refs: gram_kernel(n_all, f_all, *refs),
        out_shape=(
            jax.ShapeDtypeStruct((n_rows, n_dev), F32),
            jax.ShapeDtypeStruct((2, n_all, shard), BF16),
            jax.ShapeDtypeStruct((2, n_dev, shard), F32),
        ),
        in_specs=[smem, vmem, vmem],
        out_specs=(vmem,) * 3,
        compiler_params=params,
        name="gram",
    )(place, near, far)

    def exchange(rows, groups):
        count = len(groups[0])
        chunks = rows.reshape(count, 1, rows.shape[0] // count * n_dev)
        moved = lax.all_to_all(chunks, "f", 0, 0, axis_index_groups=groups, tiled=True)
        return moved.reshape(rows.shape)

    shares = exchange(packed, SPLIT)
    pieces = pl.pallas_call(
        share_kernel,
        out_shape=jax.ShapeDtypeStruct((n_ring * DEPTH, n_dev), F32),
        in_specs=[vmem],
        out_specs=vmem,
        compiler_params=params,
        name="share",
    )(shares)
    spread = pl.pallas_call(
        spread_kernel,
        out_shape=jax.ShapeDtypeStruct((n_split * OUT_DEPTH, n_dev), F32),
        in_specs=[smem, vmem],
        out_specs=vmem,
        compiler_params=params,
        name="spread",
    )(place, exchange(pieces, RING))
    whole = exchange(spread, SPLIT)
    grad_a, grad_b, objective = pl.pallas_call(
        lambda *refs: final_kernel(n_all, f_all, *refs),
        out_shape=(
            jax.ShapeDtypeStruct((n_dev, shard), F32),
            jax.ShapeDtypeStruct((n_dev, shard), F32),
            jax.ShapeDtypeStruct((1, 1), F32),
        ),
        in_specs=[smem] + [vmem] * 3,
        out_specs=(vmem,) * 3,
        compiler_params=params,
        name="final",
    )(place, whole, cent, base)
    return (grad_a, grad_b, objective.reshape(()))


def solution(mesh):
    n_dp, n_row, n_col = (mesh.shape[name] for name in ("dp", "row", "col"))
    flat = Mesh(mesh.devices.reshape(n_dp, n_row * n_col), ("dp", "f"))
    spec = P("dp", "f")
    return jax.shard_map(
        on_device, mesh=flat, in_specs=(spec, spec), out_specs=(spec, spec, P()), check_vma=False
    )
```

```python
import jax
import jax.numpy as jnp
from jax import lax
from jax.experimental import pallas as pl
from jax.experimental.pallas import tpu as pltpu
from jax.sharding import Mesh, PartitionSpec as P

N_X, N_Y, N_Z, N_CORE = 4, 2, 8, 2
RING_ORDER = (5, 6, 3, 2, 1, 0, 4, 7)
SPLIT_ORDER = ((2, 1, 1), (3, 1, 1), (2, 1, 0), (2, 0, 1), (1, 1, 1), (2, 0, 0), (3, 1, 0), (1, 1, 0), (0, 0, 1), (3, 0, 1), (3, 0, 0), (1, 0, 1), (1, 0, 0), (0, 0, 0), (0, 1, 1), (0, 1, 0))


def place_of(x, y, z, core):
    return ((x * N_Y + y) * N_Z + z) * N_CORE + core


SPLIT = [[place_of(x, y, z, c) for x, y, c in SPLIT_ORDER] for z in range(N_Z)]
RING = [[place_of(x, y, z, c) for z in RING_ORDER] for x, y, c in SPLIT_ORDER]
FOLD, CROSS = 4, 8
PER_VIEW = 2 * FOLD + CROSS
DEPTH = 2 * PER_VIEW + 1
OUT_VIEW = FOLD + CROSS
OUT_DEPTH = 2 * OUT_VIEW + 2
F32, BF16 = jnp.float32, jnp.bfloat16
ROW_DIMS = (((1,), (1,)), ((), ()))


def split3(value):
    first = value.astype(BF16)
    rest = value - first.astype(F32)
    second = rest.astype(BF16)
    third = (rest - second.astype(F32)).astype(BF16)
    return (first, second, third)


def iotas(shape):
    return (lax.broadcasted_iota(jnp.int32, shape, 0), lax.broadcasted_iota(jnp.int32, shape, 1))


def total_sum(value):
    return jnp.sum(value, axis=(0, 1), keepdims=True)


def col_sum(value):
    return jnp.sum(value, axis=0, keepdims=True)


def roll_half(value):
    return pltpu.roll(value, value.shape[1] // 2, 1)


def fold(gram):
    half = gram.shape[0] // 2
    top, low = gram[:half], roll_half(gram[half:])
    rows, cols = iotas(top.shape)
    return jnp.where(rows < cols, top, low)


def unfold(folded, diag):
    square = jnp.concatenate([folded, roll_half(folded)], axis=0)
    turned = square.T
    rows, cols = iotas(square.shape)
    half = square.shape[0] // 2
    first = jnp.where(rows < cols, square, jnp.where(rows == cols, diag, turned))
    second = jnp.where(rows < cols, turned, square)
    return jnp.where((rows >= half) & (cols >= half), second, first)


def put_rows(ref, depth, start, value):
    chunks = ref.shape[0] // depth
    for j in range(value.shape[0] // chunks):
        ref[pl.ds(start + j, chunks, stride=depth), :] = value[j * chunks : (j + 1) * chunks]


def take_rows(ref, depth, start, count):
    chunks = ref.shape[0] // depth
    parts = [ref[pl.ds(start + j, chunks, stride=depth), :] for j in range(count)]
    return jnp.concatenate(parts, axis=0)


def gram_kernel(n_all, f_all, place, near, far, packed, cent, base):
    @pl.when(place[0] == 0)
    def _():
        gram_body(n_all, f_all, (near, far), 0, packed, cent, base)

    @pl.when(place[0] != 0)
    def _():
        gram_body(n_all, f_all, (far, near), 1, packed, cent, base)


def gram_body(n_all, f_all, halves, plane, packed, cent, base):
    n_dev = halves[0].shape[1]
    coef = 2.0 * n_all / (25.0 * (n_all - 1))
    views = [[half[view].astype(F32) for half in halves] for view in range(2)]
    gaps = [views[0][i] - views[1][i] for i in range(2)]
    loss = jnp.zeros((1, 1), F32)
    lines = []
    for view, zs in enumerate(views):
        mean = (col_sum(zs[0]) + col_sum(zs[1])) / n_all
        diffs = [z - mean for z in zs]
        squares = col_sum(diffs[0] * diffs[0] + diffs[1] * diffs[1])
        std = jnp.sqrt(squares / (n_all - 1) + 0.0001)
        cs = [diff.astype(BF16) for diff in diffs]
        cent[view, :n_dev] = cs[0]
        cent[view, n_dev:] = cs[1]
        every = jnp.concatenate(cs, axis=0)
        top = lax.dot_general(cs[0], every, ROW_DIMS, preferred_element_type=F32)
        low = lax.dot_general(cs[1], cs[1], ROW_DIMS, preferred_element_type=F32)
        fs = [c.astype(F32) for c in cs]
        r = col_sum(fs[0] + fs[1])
        d = col_sum(fs[0] * fs[0] + fs[1] * fs[1]) / (n_all - 1)
        hinge = jnp.where(std < 1.0, n_all / (2.0 * std * (n_all - 1)), F32(0.0))
        pulled = coef * d
        rest = gaps[plane] if view == 0 else -gaps[plane]
        base[view] = rest - hinge * diffs[plane] - pulled * fs[plane] + pulled * (r / n_all)
        terms = 25.0 * jnp.maximum(1.0 - std, 0.0) - d * d
        loss = loss + total_sum(terms) / f_all
        g00, g01 = top[:, :n_dev], top[:, n_dev:]
        put_rows(packed, DEPTH, view * PER_VIEW, fold(g00))
        put_rows(packed, DEPTH, view * PER_VIEW + FOLD, fold(low))
        put_rows(packed, DEPTH, view * PER_VIEW + 2 * FOLD, g01)
        rows, cols = iotas(g00.shape)
        for block in (g00, low):
            lines.append(col_sum(jnp.where(rows == cols, block, F32(0.0))))
            lines.append(col_sum(block))
    squared_gap = total_sum(gaps[0] * gaps[0] + gaps[1] * gaps[1])
    loss = loss + (25.0 / (n_all * f_all)) * squared_gap
    rows, unused = iotas((packed.shape[0] // DEPTH, n_dev))
    extra = jnp.where(rows == len(lines), loss, F32(0.0))
    for i, line in enumerate(lines):
        extra = jnp.where(rows == i, line, extra)
    put_rows(packed, DEPTH, DEPTH - 1, extra)


def chunk_sum(shares):
    total = shares[:DEPTH]
    for i in range(1, shares.shape[0] // DEPTH):
        total = total + shares[i * DEPTH : (i + 1) * DEPTH]
    return total


def share_kernel(shares, spread):
    total = chunk_sum(shares)
    for i in range(spread.shape[0] // DEPTH):
        spread[i * DEPTH : (i + 1) * DEPTH] = total


def spread_kernel(place, shares, spread):
    total = chunk_sum(shares)
    first_plane = place[0] == 0
    pieces = []
    for view in range(2):
        start = view * PER_VIEW
        block0, block1 = total[start : start + FOLD], total[start + FOLD : start + 2 * FOLD]
        pieces.append(jnp.where(first_plane, block0, block1))
        pieces.append(total[start + 2 * FOLD : start + PER_VIEW])
    pieces.append(total[DEPTH - 1 :])
    body = total[: DEPTH - 1]
    pieces.append(2.0 * col_sum(body * body))
    chunk = jnp.concatenate(pieces, axis=0)
    for i in range(spread.shape[0] // OUT_DEPTH):
        spread[i * OUT_DEPTH : (i + 1) * OUT_DEPTH] = chunk


def final_kernel(n_all, f_all, place, packed, cent, base, grad_a, grad_b, objective):
    n_dev = base.shape[1]
    coef = 2.0 * n_all / (25.0 * (n_all - 1))
    first_plane = place[0] == 0
    extra = take_rows(packed, OUT_DEPTH, OUT_DEPTH - 2, 1)
    norms = take_rows(packed, OUT_DEPTH, OUT_DEPTH - 1, 1)
    square = total_sum(norms)
    unused, lanes = iotas((1, n_dev))
    for view, grad in enumerate((grad_a, grad_b)):
        folded = take_rows(packed, OUT_DEPTH, view * OUT_VIEW, FOLD)
        g01 = take_rows(packed, OUT_DEPTH, view * OUT_VIEW + FOLD, CROSS)
        diag0, sum0, diag1, sum1 = (extra[4 * view + i : 4 * view + i + 1] for i in range(4))
        diags = diag0 * diag0 + diag1 * diag1
        square = square + total_sum(jnp.where(lanes < n_dev // 2, diags, -diags))
        block = unfold(folded, jnp.where(first_plane, diag0, diag1))
        g10 = g01.T
        v0 = (sum0 + col_sum(g10)) / n_all
        v1 = (sum1 + col_sum(g01)) / n_all
        left = jnp.where(first_plane, block, g10) - v0
        right = jnp.where(first_plane, g01, block) - v1
        parts = jnp.concatenate(split3(jnp.concatenate([left, right], axis=1)), axis=0)
        pulls = jnp.dot(parts, cent[view], preferred_element_type=F32)
        pull = pulls[:n_dev] + pulls[n_dev : 2 * n_dev] + pulls[2 * n_dev :]
        grad[...] = base[view] + (coef / (n_all - 1)) * pull
    loss = extra[8:9, 0:1] + square / (float(n_all - 1) * float(n_all - 1) * f_all)
    objective[...] = loss * n_all / (50.0 * f_all)


def on_device(view_a, view_b):
    n_dp = lax.axis_size("dp")
    n_split, n_ring = len(SPLIT_ORDER), len(RING_ORDER)
    n_dev, shard = view_a.shape
    n_all = n_dev * n_dp
    f_all = shard * n_split * n_ring
    swap = [(0, 1), (1, 0)]
    vmem = pl.BlockSpec(memory_space=pltpu.VMEM)
    smem = pl.BlockSpec(memory_space=pltpu.SMEM)
    params = pltpu.CompilerParams(vmem_limit_bytes=32 * 1024 * 1024)
    place = lax.axis_index("dp").astype(jnp.int32).reshape(1)
    near = jnp.stack([view_a, view_b])
    far = lax.ppermute(near, "dp", swap)
    n_rows = n_split * DEPTH
    packed, cent, base = pl.pallas_call(
        lambda *refs: gram_kernel(n_all, f_all, *refs),
        out_shape=(
            jax.ShapeDtypeStruct((n_rows, n_dev), F32),
            jax.ShapeDtypeStruct((2, n_all, shard), BF16),
            jax.ShapeDtypeStruct((2, n_dev, shard), F32),
        ),
        in_specs=[smem, vmem, vmem],
        out_specs=(vmem,) * 3,
        compiler_params=params,
        name="gram",
    )(place, near, far)

    def exchange(rows, groups):
        count = len(groups[0])
        chunks = rows.reshape(count, 1, rows.shape[0] // count * n_dev)
        moved = lax.all_to_all(chunks, "f", 0, 0, axis_index_groups=groups, tiled=True)
        return moved.reshape(rows.shape)

    shares = exchange(packed, SPLIT)
    pieces = pl.pallas_call(
        share_kernel,
        out_shape=jax.ShapeDtypeStruct((n_ring * DEPTH, n_dev), F32),
        in_specs=[vmem],
        out_specs=vmem,
        compiler_params=params,
        name="share",
    )(shares)
    spread = pl.pallas_call(
        spread_kernel,
        out_shape=jax.ShapeDtypeStruct((n_split * OUT_DEPTH, n_dev), F32),
        in_specs=[smem, vmem],
        out_specs=vmem,
        compiler_params=params,
        name="spread",
    )(place, exchange(pieces, RING))
    whole = exchange(spread, SPLIT)
    grad_a, grad_b, objective = pl.pallas_call(
        lambda *refs: final_kernel(n_all, f_all, *refs),
        out_shape=(
            jax.ShapeDtypeStruct((n_dev, shard), F32),
            jax.ShapeDtypeStruct((n_dev, shard), F32),
            jax.ShapeDtypeStruct((1, 1), F32),
        ),
        in_specs=[smem] + [vmem] * 3,
        out_specs=(vmem,) * 3,
        compiler_params=params,
        name="final",
    )(place, whole, cent, base)
    return (grad_a, grad_b, objective.reshape(()))


def solution(mesh):
    n_dp, n_row, n_col = (mesh.shape[name] for name in ("dp", "row", "col"))
    flat = Mesh(mesh.devices.reshape(n_dp, n_row * n_col), ("dp", "f"))
    spec = P("dp", "f")
    return jax.shard_map(
        on_device, mesh=flat, in_specs=(spec, spec), out_specs=(spec, spec, P()), check_vma=False
    )
```
